32 devices in a mesh: ctx: 16 (over z, y, core), fsdp: 2 (over x).
Axes of the slice: x: 2, y: 2, z: 4, core: 2. Of those that a mesh axis runs over, the one named last changes fastest.
Arguments:
- query_proj: bfloat16 [8192, 4096], P('ctx', 'fsdp'), may hold values from -6 to 6
- key_proj: bfloat16 [8192, 4096], P('ctx', 'fsdp'), may hold values from -6 to 6
- value_proj: bfloat16 [8192, 4096], P('ctx', 'fsdp'), may hold values from -6 to 6
- filters: bfloat16 [4096, 128], P('fsdp'), may hold values from -0.5 to 0.5
- out_weight: bfloat16 [4096, 4096], P('fsdp', 'ctx'), may hold values from -0.09375 to 0.09375
- cotangent: bfloat16 [8192, 4096], P('ctx', 'fsdp'), may hold values from -6 to 6
Outputs:
- output: bfloat16 [8192, 4096], P('ctx', 'fsdp')
- grad_query: bfloat16 [8192, 4096], P('ctx', 'fsdp')
- grad_key: bfloat16 [8192, 4096], P('ctx', 'fsdp')
- grad_value: bfloat16 [8192, 4096], P('ctx', 'fsdp')
- grad_weight: float32 [4096, 4096], P('fsdp', 'ctx')
- grad_filters: float32 [4096, 128], P(('fsdp', 'ctx'))
The draws below stay inside these ranges and needn't reach their ends.
All inputs are finite; a program needn't handle non-finite values.
Results may differ from the reference program's by a relative error of at most 0.0065.
Values may be sent and summed in bfloat16 or wider, within the bound.
A program may use at most 192 MiB of HBM per device.

```python
import math
import jax
import jax.numpy as jnp
from jax import lax

D = 4096
C = 4096
L = 128
SEQ = 8192


def with_spikes(drawn, stream_key, source, target, parts, factor):
    def block_of(dim):
        return (jnp.arange(drawn.shape[dim]) // (drawn.shape[dim] // parts)).reshape((-1,) + (1,) * (drawn.ndim - 1 - dim))

    first = jax.random.permutation(stream_key, parts)[block_of(target)]
    second = (block_of(target) + parts // 2) % parts
    return jnp.where((block_of(source) == first) | (block_of(source) == second), factor * drawn, drawn)


def block_scale(stream_key, shape, pieces, smallest, high):
    def one(dim, shards_of):
        draws = jax.random.uniform(jax.random.fold_in(jax.random.fold_in(stream_key, 6), dim), (shards_of,), jnp.float32, smallest / len(pieces), high / len(pieces))
        return jnp.repeat(jnp.exp(draws), shape[dim] // shards_of).reshape((-1,) + (1,) * (len(shape) - dim - 1))

    factor_of = one(*pieces[0])
    for cut in pieces[1:]:
        factor_of = factor_of * one(*cut)
    return factor_of


def centred(stream_key, shape, spread, bound, shards=(), held_as=jnp.bfloat16):
    factor_of = block_scale(stream_key, shape, shards, -0.22, 0.18) if shards else 1.0
    values = jax.random.normal(stream_key, shape, jnp.float32) * spread * factor_of
    return jnp.minimum(jnp.maximum(values, -bound), bound).astype(held_as)


def heavy_noise(key, extent, deviation, reach, cuts, heavy, held_as=jnp.bfloat16):
    drawn = deviation * jax.random.normal(key, extent, jnp.float32)
    if cuts:
        drawn = drawn * block_scale(key, extent, cuts, -0.22, 0.18)
    return jnp.clip(with_spikes(drawn, jax.random.fold_in(key, 3), *heavy), -reach, reach).astype(held_as)


def setup_inputs(seed: int = 0) -> dict:
    keys = jax.random.split(jax.random.key(seed), 7)
    query_proj = centred(keys[0], (SEQ, C), 1.0, 6.0, ((0, 16), (1, 2)))
    key_proj = centred(keys[1], (SEQ, C), 1.0, 6.0, ((0, 16), (1, 2)))
    value_proj = centred(keys[2], (SEQ, C), 1.0, 6.0, ((0, 16), (1, 2)))
    filters = centred(keys[3], (C, L), L ** -0.5, 0.5, ((0, 2),))
    out_weight = centred(keys[4], (C, D), C ** -0.5, 0.09375, ((0, 2), (1, 16)))
    cotangent = heavy_noise(keys[5], (SEQ, D), 1.0, 6.0, ((0, 16), (1, 2)), (0, 1, 16, 2.0))
    return dict(query_proj=query_proj, key_proj=key_proj, value_proj=value_proj, filters=filters, out_weight=out_weight, cotangent=cotangent)


def causal_group(taps_rows, series):
    padded = jnp.pad(series, ((0, 0), (L - 1, 0)))

    def step(tap_index, running):
        window = lax.dynamic_slice_in_dim(padded, L - 1 - tap_index, SEQ, 1)
        return running + taps_rows[:, tap_index][:, None] * window
    return lax.fori_loop(0, L, step, jnp.zeros_like(series))

def anti_group(taps_rows, series):
    padded = jnp.pad(series, ((0, 0), (0, L - 1)))

    def step(tap_index, running):
        window = lax.dynamic_slice_in_dim(padded, tap_index, SEQ, 1)
        return running + taps_rows[:, tap_index][:, None] * window
    return lax.fori_loop(0, L, step, jnp.zeros_like(series))

def taps_group(grads, series):
    padded = jnp.pad(series, ((0, 0), (L - 1, 0)))

    def step(tap_index, running):
        window = lax.dynamic_slice_in_dim(padded, L - 1 - tap_index, SEQ, 1)
        return running.at[:, tap_index].set(lax.optimization_barrier(jnp.sum(grads * window, axis=1)))
    return lax.fori_loop(0, L, step, jnp.zeros((grads.shape[0], L), grads.dtype))

def reference(query_proj, key_proj, value_proj, filters, out_weight, cotangent):
    group_size = math.gcd(C, 256)
    scale = 1.0 / math.sqrt(SEQ)
    product = (key_proj.astype(jnp.float32) * value_proj.astype(jnp.float32)).astype(jnp.bfloat16)
    product_f = lax.optimization_barrier(product).astype(jnp.float32)
    series = product_f.T.reshape(C // group_size, group_size, SEQ)
    taps_rows = filters.astype(jnp.float32).reshape(C // group_size, group_size, L)
    mixed_t = lax.map(lambda members: causal_group(members[0], members[1]), (taps_rows, series))
    mixed = mixed_t.reshape(C, SEQ).T.astype(jnp.bfloat16)
    mixed_f = lax.optimization_barrier(mixed).astype(jnp.float32)
    gated = (query_proj.astype(jnp.float32) * mixed_f).astype(jnp.bfloat16)
    output = jnp.dot(gated, out_weight, preferred_element_type=jnp.float32).astype(jnp.bfloat16)
    grad_gated = jnp.dot(cotangent, out_weight.T, preferred_element_type=jnp.float32)
    grad_query = (grad_gated * mixed_f).astype(jnp.bfloat16)
    grad_mixed = (grad_gated * query_proj.astype(jnp.float32)).astype(jnp.bfloat16)
    grad_series = lax.optimization_barrier(grad_mixed).astype(jnp.float32).T.reshape(C // group_size, group_size, SEQ)
    back_t = lax.map(lambda members: anti_group(members[0], members[1]), (taps_rows, grad_series))
    grad_product = back_t.reshape(C, SEQ).T.astype(jnp.bfloat16)
    grad_product_f = lax.optimization_barrier(grad_product).astype(jnp.float32)
    grad_key = (grad_product_f * value_proj.astype(jnp.float32)).astype(jnp.bfloat16)
    grad_value = (grad_product_f * key_proj.astype(jnp.float32)).astype(jnp.bfloat16)
    grad_weight = jnp.dot(gated.T, cotangent, preferred_element_type=jnp.float32) * scale
    tap_sums = lax.map(lambda members: taps_group(members[0], members[1]), (grad_series, series))
    grad_filters = tap_sums.reshape(C, L) * scale
    return (output, grad_query, grad_key, grad_value, grad_weight, grad_filters)
```

```python
import functools
import math

import jax
import jax.numpy as jnp
from jax import lax
from jax.experimental import pallas as pl
from jax.experimental.pallas import tpu as pltpu
from jax.sharding import PartitionSpec as P

TAPS = 8
ROWS = 16
HALVES = 2
F32 = jnp.float32
BF16 = jnp.bfloat16


def tree_sum(terms):
    while len(terms) > 1:
        terms = [terms[i] + terms[i + 1] for i in range(0, len(terms), 2)]
    return terms[0]


def fill(dst, start, src):
    count = src.shape[0]

    def body(i, carry):
        dst[pl.ds(start + i * 16, 16)] = src[pl.ds(i * 16, 16)]
        return carry

    lax.fori_loop(0, count // 16, body, 0)


def fir(held, f_ref, o_ref, base, sign):
    tokens, lanes = o_ref.shape[0], o_ref.shape[1:]
    taps = f_ref.shape[0]

    def token_block(tb, carry):
        t0 = tb * ROWS

        def tap_block(jb, totals):
            j0 = jb * TAPS
            fs = [f_ref[j0 + u] for u in range(TAPS)]
            low = base + t0 + sign * j0 - (TAPS - 1 if sign < 0 else 0)
            xs = [held[low + k] for k in range(ROWS + TAPS - 1)]
            new = []
            for i in range(ROWS):
                if sign < 0:
                    terms = [fs[u] * xs[i + TAPS - 1 - u] for u in range(TAPS)]
                else:
                    terms = [fs[u] * xs[i + u] for u in range(TAPS)]
                new.append(totals[i] + tree_sum(terms).astype(F32))
            return tuple(new)

        totals = lax.fori_loop(
            0, taps // TAPS, tap_block, tuple(jnp.zeros(lanes, F32) for _ in range(ROWS))
        )
        for i in range(ROWS):
            o_ref[t0 + i] = totals[i].astype(BF16)
        return carry

    lax.fori_loop(0, tokens // ROWS, token_block, 0)


def mix_kernel(x_ref, h_ref, f_ref, o_ref, held):
    taps = h_ref.shape[0]
    fill(held, 0, h_ref)
    fill(held, taps, x_ref)
    fir(held, f_ref, o_ref, taps, -1)


def back_kernel(g_ref, h_ref, f_ref, o_ref, held):
    fill(held, 0, g_ref)
    fill(held, g_ref.shape[0], h_ref)
    fir(held, f_ref, o_ref, 0, 1)


def tap_kernel(x_ref, h_ref, g_ref, o_ref, held):
    taps, tokens, lanes = h_ref.shape[0], g_ref.shape[0], g_ref.shape[1:]
    fill(held, 0, h_ref)
    fill(held, taps, x_ref)

    def tap_block(jb, carry):
        j0 = jb * ROWS

        def token_block(tb, totals):
            t0 = tb * TAPS
            gs = [g_ref[t0 + u] for u in range(TAPS)]
            low = taps + t0 - j0 - (ROWS - 1)
            xs = [held[low + k] for k in range(ROWS + TAPS - 1)]
            new = []
            for i in range(ROWS):
                terms = [gs[u] * xs[u - i + ROWS - 1] for u in range(TAPS)]
                new.append(totals[i] + tree_sum(terms).astype(F32))
            return tuple(new)

        totals = lax.fori_loop(
            0, tokens // TAPS, token_block, tuple(jnp.zeros(lanes, F32) for _ in range(ROWS))
        )
        for i in range(ROWS):
            o_ref[j0 + i] = totals[i]
        return carry

    lax.fori_loop(0, taps // ROWS, tap_block, 0)


def conv_call(kernel, series, halo, third, out_shape):
    whole = pl.BlockSpec(memory_space=pltpu.VMEM)
    lanes = series.shape[1:]
    macs = series.shape[0] * halo.shape[0] * lanes[0] * lanes[1]
    return pl.pallas_call(
        kernel,
        out_shape=out_shape,
        in_specs=[whole] * 3,
        out_specs=whole,
        scratch_shapes=[pltpu.VMEM((series.shape[0] + halo.shape[0],) + lanes, BF16)],
        compiler_params=pltpu.CompilerParams(vmem_limit_bytes=32 * 2**20),
        cost_estimate=pl.CostEstimate(
            flops=macs * 150, bytes_accessed=6 * series.size, transcendentals=0
        ),
    )(series, halo, third)


def on_device(query_proj, key_proj, value_proj, filters, out_weight, cotangent):
    tokens, channels = query_proj.shape
    taps = filters.shape[1]
    parts = lax.axis_size("ctx")
    fs = lax.axis_size("fsdp")
    features = out_weight.shape[1] * parts
    block = out_weight.shape[1]
    scale = 1.0 / math.sqrt(tokens * parts)
    me = lax.axis_index("ctx")
    fme = lax.axis_index("fsdp")
    chips = parts // 2
    chip, core = me // 2, me % 2

    order = list(range(0, chips, 2)) + list(range(1, chips, 2))[::-1]
    place = [order.index(c) for c in range(chips)]
    order_of = jnp.array(order, jnp.int32)
    pos = jnp.array(place, jnp.int32)[chip]
    step_of = jnp.where(core == 0, 1, -1)
    ring = []
    for c in range(chips):
        ring.append((2 * c, 2 * order[(place[c] + 1) % chips]))
        ring.append((2 * c + 1, 2 * order[(place[c] - 1) % chips] + 1))
    pair = [(i, i ^ 1) for i in range(parts)]

    def sibling(x):
        return lax.ppermute(x, "ctx", pair)

    def around(x):
        return lax.ppermute(x, "ctx", ring)

    fring = [(i, (i + 1) % fs) for i in range(fs)]
    cots = [cotangent]
    for _ in range(fs - 1):
        cots.append(lax.ppermute(cots[-1], "fsdp", fring))

    lanes = (channels // 128, 128)
    f3 = filters.T.reshape((taps,) + lanes)
    product = (key_proj.astype(F32) * value_proj.astype(F32)).astype(BF16)
    x3 = product.reshape((tokens,) + lanes)
    up = [(i, i + 1) for i in range(parts - 1)]
    down = [(i + 1, i) for i in range(parts - 1)]
    x_halo = lax.ppermute(product[tokens - taps :], "ctx", up).reshape((taps,) + lanes)

    whole_weight = jnp.zeros((channels, features), BF16)
    half_rows = channels // HALVES
    mine = [out_weight[h * half_rows : (h + 1) * half_rows] for h in range(HALVES)]
    for s in range(chips):
        source = order_of[(pos - s * step_of) % chips]
        other = order_of[(pos + s * step_of) % chips]
        for h in range(HALVES):
            theirs = sibling(mine[h])
            whole_weight = lax.dynamic_update_slice(
                whole_weight, mine[h], (h * half_rows, (source * 2 + core) * block)
            )
            whole_weight = lax.dynamic_update_slice(
                whole_weight, theirs, (h * half_rows, (other * 2 + 1 - core) * block)
            )
            if s < chips - 1:
                mine[h] = around(mine[h])

    mixed3 = conv_call(
        mix_kernel, x3, x_halo, f3, jax.ShapeDtypeStruct((tokens,) + lanes, BF16)
    )
    mixed_f = mixed3.reshape(tokens, channels).astype(F32)
    query_f = query_proj.astype(F32)
    gated = (query_f * mixed_f).astype(BF16)

    full_cot = jnp.zeros((tokens, features), BF16)
    for i, piece in enumerate(cots):
        full_cot = lax.dynamic_update_slice(
            full_cot, piece, (0, ((fme - i) % fs) * piece.shape[1])
        )

    split_cot = full_cot.reshape(tokens, chips, 2, block)
    keep = lax.dynamic_index_in_dim(split_cot, core, 2, keepdims=False)
    give = lax.dynamic_index_in_dim(split_cot, 1 - core, 2, keepdims=False)
    cot_cols = jnp.concatenate([keep, sibling(give)], 0).reshape(2 * tokens, chips * block)
    gated_pair = jnp.concatenate([gated, sibling(gated)], 0)

    sums = [None] * HALVES
    for s in range(chips):
        dest = order_of[(pos - (1 + s) * step_of) % chips]
        cols = lax.dynamic_slice(cot_cols, (0, dest * block), (2 * tokens, block))
        for h in range(HALVES):
            rows = gated_pair[:, h * half_rows : (h + 1) * half_rows]
            term = lax.dot_general(
                rows, cols, (((0,), (0,)), ((), ())), preferred_element_type=F32
            )
            if s:
                term = term + sums[h].astype(F32)
            sums[h] = around(term.astype(BF16)) if s < chips - 1 else term
    grad_weight = jnp.concatenate(sums, 0) * scale

    grad_gated = lax.dot_general(
        full_cot, whole_weight, (((1,), (1,)), ((), ())), preferred_element_type=F32
    )
    grad_query = (grad_gated * mixed_f).astype(BF16)
    grad_mixed = (grad_gated * query_f).astype(BF16)
    g3 = grad_mixed.reshape((tokens,) + lanes)
    g_halo = lax.ppermute(grad_mixed[:taps], "ctx", down).reshape((taps,) + lanes)
    tap3 = conv_call(tap_kernel, x3, x_halo, g3, jax.ShapeDtypeStruct((taps,) + lanes, F32))
    grad_filters = (
        lax.psum_scatter(
            tap3.reshape(taps, channels).T, "ctx", scatter_dimension=0, tiled=True
        )
        * scale
    )
    back3 = conv_call(
        back_kernel, g3, g_halo, f3, jax.ShapeDtypeStruct((tokens,) + lanes, BF16)
    )
    grad_product_f = back3.reshape(tokens, channels).astype(F32)
    grad_key = (grad_product_f * value_proj.astype(F32)).astype(BF16)
    grad_value = (grad_product_f * key_proj.astype(F32)).astype(BF16)

    own = features // fs
    running = None
    for s in range(fs):
        dest = (fme - 1 - s) % fs
        columns = lax.dynamic_slice(whole_weight, (0, dest * own), (channels, own))
        value = jnp.dot(gated, columns, preferred_element_type=F32)
        if s:
            value = value + running.astype(F32)
        if s < fs - 1:
            running = lax.ppermute(value.astype(BF16), "fsdp", fring)
    output = value.astype(BF16)
    return (output, grad_query, grad_key, grad_value, grad_weight, grad_filters)


def solution(mesh):
    in_specs = (
        P("ctx", "fsdp"),
        P("ctx", "fsdp"),
        P("ctx", "fsdp"),
        P("fsdp", None),
        P("fsdp", "ctx"),
        P("ctx", "fsdp"),
    )
    out_specs = (
        P("ctx", "fsdp"),
        P("ctx", "fsdp"),
        P("ctx", "fsdp"),
        P("ctx", "fsdp"),
        P("fsdp", "ctx"),
        P(("fsdp", "ctx"), None),
    )
    return jax.shard_map(
        on_device, mesh=mesh, in_specs=in_specs, out_specs=out_specs, check_vma=False
    )
```

```python
import functools
import math

import jax
import jax.numpy as jnp
from jax import lax
from jax.experimental import pallas as pl
from jax.experimental.pallas import tpu as pltpu
from jax.sharding import PartitionSpec as P

TAPS = 8
ROWS = 16
HALVES = 2
F32 = jnp.float32
BF16 = jnp.bfloat16


def tree_sum(terms):
    while len(terms) > 1:
        terms = [terms[i] + terms[i + 1] for i in range(0, len(terms), 2)]
    return terms[0]


def fill(dst, start, src):
    count = src.shape[0]

    def body(i, carry):
        dst[pl.ds(start + i * 16, 16)] = src[pl.ds(i * 16, 16)]
        return carry

    lax.fori_loop(0, count // 16, body, 0)


def fir(held, f_ref, o_ref, base, sign):
    tokens, lanes = o_ref.shape[0], o_ref.shape[1:]
    taps = f_ref.shape[0]

    def token_block(tb, carry):
        t0 = tb * ROWS

        def tap_block(jb, totals):
            j0 = jb * TAPS
            fs = [f_ref[j0 + u] for u in range(TAPS)]
            low = base + t0 + sign * j0 - (TAPS - 1 if sign < 0 else 0)
            xs = [held[low + k] for k in range(ROWS + TAPS - 1)]
            new = []
            for i in range(ROWS):
                if sign < 0:
                    terms = [fs[u] * xs[i + TAPS - 1 - u] for u in range(TAPS)]
                else:
                    terms = [fs[u] * xs[i + u] for u in range(TAPS)]
                new.append(totals[i] + tree_sum(terms).astype(F32))
            return tuple(new)

        totals = lax.fori_loop(
            0, taps // TAPS, tap_block, tuple(jnp.zeros(lanes, F32) for _ in range(ROWS))
        )
        for i in range(ROWS):
            o_ref[t0 + i] = totals[i].astype(BF16)
        return carry

    lax.fori_loop(0, tokens // ROWS, token_block, 0)


def mix_kernel(x_ref, h_ref, f_ref, o_ref, held):
    taps = h_ref.shape[0]
    fill(held, 0, h_ref)
    fill(held, taps, x_ref)
    fir(held, f_ref, o_ref, taps, -1)


def back_kernel(g_ref, h_ref, f_ref, o_ref, held):
    fill(held, 0, g_ref)
    fill(held, g_ref.shape[0], h_ref)
    fir(held, f_ref, o_ref, 0, 1)


def tap_kernel(x_ref, h_ref, g_ref, o_ref, held):
    taps, tokens, lanes = h_ref.shape[0], g_ref.shape[0], g_ref.shape[1:]
    fill(held, 0, h_ref)
    fill(held, taps, x_ref)

    def tap_block(jb, carry):
        j0 = jb * ROWS

        def token_block(tb, totals):
            t0 = tb * TAPS
            gs = [g_ref[t0 + u] for u in range(TAPS)]
            low = taps + t0 - j0 - (ROWS - 1)
            xs = [held[low + k] for k in range(ROWS + TAPS - 1)]
            new = []
            for i in range(ROWS):
                terms = [gs[u] * xs[u - i + ROWS - 1] for u in range(TAPS)]
                new.append(totals[i] + tree_sum(terms).astype(F32))
            return tuple(new)

        totals = lax.fori_loop(
            0, tokens // TAPS, token_block, tuple(jnp.zeros(lanes, F32) for _ in range(ROWS))
        )
        for i in range(ROWS):
            o_ref[j0 + i] = totals[i]
        return carry

    lax.fori_loop(0, taps // ROWS, tap_block, 0)


def conv_call(kernel, series, halo, third, out_shape):
    whole = pl.BlockSpec(memory_space=pltpu.VMEM)
    lanes = series.shape[1:]
    macs = series.shape[0] * halo.shape[0] * lanes[0] * lanes[1]
    return pl.pallas_call(
        kernel,
        out_shape=out_shape,
        in_specs=[whole] * 3,
        out_specs=whole,
        scratch_shapes=[pltpu.VMEM((series.shape[0] + halo.shape[0],) + lanes, BF16)],
        compiler_params=pltpu.CompilerParams(vmem_limit_bytes=32 * 2**20),
        cost_estimate=pl.CostEstimate(
            flops=macs * 150, bytes_accessed=6 * series.size, transcendentals=0
        ),
    )(series, halo, third)


def on_device(query_proj, key_proj, value_proj, filters, out_weight, cotangent):
    tokens, channels = query_proj.shape
    taps = filters.shape[1]
    parts = lax.axis_size("ctx")
    fs = lax.axis_size("fsdp")
    features = out_weight.shape[1] * parts
    block = out_weight.shape[1]
    scale = 1.0 / math.sqrt(tokens * parts)
    me = lax.axis_index("ctx")
    fme = lax.axis_index("fsdp")
    chips = parts // 2
    chip, core = me // 2, me % 2

    order = list(range(0, chips, 2)) + list(range(1, chips, 2))[::-1]
    place = [order.index(c) for c in range(chips)]
    order_of = jnp.array(order, jnp.int32)
    pos = jnp.array(place, jnp.int32)[chip]
    step_of = jnp.where(core == 0, 1, -1)
    ring = []
    for c in range(chips):
        ring.append((2 * c, 2 * order[(place[c] + 1) % chips]))
        ring.append((2 * c + 1, 2 * order[(place[c] - 1) % chips] + 1))
    pair = [(i, i ^ 1) for i in range(parts)]

    def sibling(x):
        return lax.ppermute(x, "ctx", pair)

    def around(x):
        return lax.ppermute(x, "ctx", ring)

    fring = [(i, (i + 1) % fs) for i in range(fs)]
    cots = [cotangent]
    for _ in range(fs - 1):
        cots.append(lax.ppermute(cots[-1], "fsdp", fring))

    lanes = (channels // 128, 128)
    f3 = filters.T.reshape((taps,) + lanes)
    product = (key_proj.astype(F32) * value_proj.astype(F32)).astype(BF16)
    x3 = product.reshape((tokens,) + lanes)
    up = [(i, i + 1) for i in range(parts - 1)]
    down = [(i + 1, i) for i in range(parts - 1)]
    x_halo = lax.ppermute(product[tokens - taps :], "ctx", up).reshape((taps,) + lanes)

    pieces = tokens // taps

    def piece(series, i):
        return series[i * taps : (i + 1) * taps]

    def call(kernel, series, halo, third, dtype):
        return conv_call(kernel, series, halo, third, jax.ShapeDtypeStruct((taps,) + lanes, dtype))

    zero, x3 = lax.optimization_barrier((jnp.zeros((), BF16), x3))
    whole_weight = jnp.broadcast_to(zero, (channels, features))
    half_rows = channels // HALVES
    mine = [out_weight[h * half_rows : (h + 1) * half_rows] for h in range(HALVES)]
    mine = list(lax.optimization_barrier(mine))
    mixed_pieces = [None] * pieces
    todo = list(range(1, pieces)) + [0]
    for s in range(chips):
        source = order_of[(pos - s * step_of) % chips]
        other = order_of[(pos + s * step_of) % chips]
        now = []
        if s >= 1:
            left = chips - 1 - s
            count = len(todo) if left <= 0 else min(1, len(todo))
            now, todo = todo[:count], todo[count:]
        inputs = [(piece(x3, i), x_halo if i == 0 else piece(x3, i - 1)) for i in now]
        if now:
            mine, inputs = lax.optimization_barrier((mine, inputs))
        held = mine
        if s < chips - 1:
            mine = [around(m) for m in held]
        made = [call(mix_kernel, a, b, f3, BF16) for a, b in inputs]
        if now and s < chips - 1:
            mine, made = lax.optimization_barrier((mine, made))
        for i, m in zip(now, made):
            mixed_pieces[i] = m
        for h in range(HALVES):
            theirs = sibling(held[h])
            whole_weight = lax.dynamic_update_slice(
                whole_weight, held[h], (h * half_rows, (source * 2 + core) * block)
            )
            whole_weight = lax.dynamic_update_slice(
                whole_weight, theirs, (h * half_rows, (other * 2 + 1 - core) * block)
            )

    mixed3 = jnp.concatenate(mixed_pieces, 0)
    mixed_f = mixed3.reshape(tokens, channels).astype(F32)
    query_f = query_proj.astype(F32)
    gated = (query_f * mixed_f).astype(BF16)

    full_cot = jnp.zeros((tokens, features), BF16)
    for i, cot in enumerate(cots):
        full_cot = lax.dynamic_update_slice(
            full_cot, cot, (0, ((fme - i) % fs) * cot.shape[1])
        )

    split_cot = full_cot.reshape(tokens, chips, 2, block)
    keep = lax.dynamic_index_in_dim(split_cot, core, 2, keepdims=False)
    give = lax.dynamic_index_in_dim(split_cot, 1 - core, 2, keepdims=False)
    cot_cols = jnp.concatenate([keep, sibling(give)], 0).reshape(2 * tokens, chips * block)
    gated_pair = jnp.concatenate([gated, sibling(gated)], 0)

    grad_gated = lax.dot_general(
        full_cot, whole_weight, (((1,), (1,)), ((), ())), preferred_element_type=F32
    )
    grad_query = (grad_gated * mixed_f).astype(BF16)
    grad_mixed = (grad_gated * query_f).astype(BF16)
    g3 = grad_mixed.reshape((tokens,) + lanes)
    g_halo = lax.ppermute(grad_mixed[:taps], "ctx", down).reshape((taps,) + lanes)

    jobs = []
    for i in range(pieces):
        before = x_halo if i == 0 else piece(x3, i - 1)
        jobs.append((tap_kernel, (piece(x3, i), before, piece(g3, i)), F32))
    for i in range(pieces):
        after = g_halo if i == pieces - 1 else piece(g3, i + 1)
        jobs.append((back_kernel, (piece(g3, i), after, f3), BF16))

    results = []
    sums = [None] * HALVES
    for s in range(chips):
        dest = order_of[(pos - (1 + s) * step_of) % chips]
        cols = lax.dynamic_slice(cot_cols, (0, dest * block), (2 * tokens, block))
        for h in range(HALVES):
            rows = gated_pair[:, h * half_rows : (h + 1) * half_rows]
            term = lax.dot_general(
                rows, cols, (((0,), (0,)), ((), ())), preferred_element_type=F32
            )
            sums[h] = term + sums[h].astype(F32) if s else term
        if s < chips - 1:
            sent = [t.astype(BF16) for t in sums]
            todo = [] if s == 0 else jobs[len(results) : len(results) + 1]
            inputs = [arrays for _, arrays, _ in todo]
            if todo:
                sent, inputs = lax.optimization_barrier((sent, inputs))
            sums = [around(t) for t in sent]
            made = [call(k, *arrays, t) for (k, _, t), arrays in zip(todo, inputs)]
            if todo:
                sums, made = lax.optimization_barrier((sums, made))
            results += made
            if len(results) == pieces and todo:
                tap_rows = functools.reduce(jnp.add, results).reshape(taps, channels).T
                sums, tap_rows = lax.optimization_barrier((sums, tap_rows))
            if s == chips - 2:
                rest = [arrays for _, arrays, _ in jobs[len(results) :]]
                sums, rest = lax.optimization_barrier((sums, rest))
    grad_weight = jnp.concatenate(sums, 0) * scale
    results += [
        call(k, *arrays, t) for (k, _, t), arrays in zip(jobs[len(results) :], rest)
    ]
    grad_filters = lax.psum_scatter(tap_rows, "ctx", scatter_dimension=0, tiled=True) * scale
    back3 = jnp.concatenate(results[pieces:], 0)
    grad_product_f = back3.reshape(tokens, channels).astype(F32)
    grad_key = (grad_product_f * value_proj.astype(F32)).astype(BF16)
    grad_value = (grad_product_f * key_proj.astype(F32)).astype(BF16)

    own = features // fs
    running = None
    for s in range(fs):
        dest = (fme - 1 - s) % fs
        columns = lax.dynamic_slice(whole_weight, (0, dest * own), (channels, own))
        value = jnp.dot(gated, columns, preferred_element_type=F32)
        if s:
            value = value + running.astype(F32)
        if s < fs - 1:
            running = lax.ppermute(value.astype(BF16), "fsdp", fring)
    output = value.astype(BF16)
    return (output, grad_query, grad_key, grad_value, grad_weight, grad_filters)


def solution(mesh):
    in_specs = (
        P("ctx", "fsdp"),
        P("ctx", "fsdp"),
        P("ctx", "fsdp"),
        P("fsdp", None),
        P("fsdp", "ctx"),
        P("ctx", "fsdp"),
    )
    out_specs = (
        P("ctx", "fsdp"),
        P("ctx", "fsdp"),
        P("ctx", "fsdp"),
        P("ctx", "fsdp"),
        P("fsdp", "ctx"),
        P(("fsdp", "ctx"), None),
    )
    return jax.shard_map(
        on_device, mesh=mesh, in_specs=in_specs, out_specs=out_specs, check_vma=False
    )
```
